128 devices in a mesh: frame: 64 (over x, z, y), head: 2 (over core).
Axes of the slice: x: 4, y: 4, z: 4, core: 2. Of those that a mesh axis runs over, the one named last changes fastest.
Arguments:
- queries: bfloat16 [32768, 3072], P('frame', 'head'), may hold values from -8 to 8
- key_rows: bfloat16 [32768, 3072], P('frame', 'head'), may hold values from -8 to 8
- value_rows: bfloat16 [32768, 3072], P('frame', 'head'), may hold values from -6 to 6
- block_mask: int32 [512, 32], P('frame'), may hold values from -1 to 511, as said below
- out_weight: bfloat16 [3072, 3072], P('head'), may hold values from -0.109375 to 0.109375
Outputs:
- attended: bfloat16 [32768, 3072], P(('frame', 'head'))
The draws below stay inside these ranges and needn't reach their ends.
Inputs may be any that keep to these rules, and one draw needn't show every extreme that they name: `block_mask`: row f * 8 + b belongs to block b of frame f. Its first 8 entries are the blocks of frame f in order. Entry 8 + 4 k + 2 s + r, for k below 6 and r of 0 and 1, names a block of frame f - 2^k (s = 0) or f + 2^k (s = 1), or is -1 exactly when that frame lies outside the clip; its two entries r differ. Over the 8 rows of one frame, the entries of one k and s name exactly max(2, 8 // 2^k) different blocks.
All inputs are finite; a program needn't handle non-finite values.
Results may differ from the reference program's by a relative error of at most 0.0058.
Values may be sent and summed in bfloat16 or wider, within the bound.
No kernel may reach another device: no remote copies, remote signals or barrier semaphores. Data moves between devices by JAX's collectives and lax.ppermute only.
A program may use at most 192 MiB of HBM per device.

```python
import math
import jax
import jax.numpy as jnp
from jax import lax

D = 3072
HEADS = 24
HD = 128
BLK = 64
BLK_F = 8
LEVELS = 6
TOKENS = 32768
QBLOCKS = 512
SLOTS = 32


def draw_queries(key, part):
    key = jax.random.fold_in(key, 31)
    base = jnp.clip(jax.random.normal(key, (TOKENS, HEADS * HD), jnp.float32), -8.0, 8.0)
    return base.astype(jnp.bfloat16)


def draw_key_rows(key, part):
    key = jax.random.fold_in(key, 32)
    base = jnp.clip(jax.random.normal(key, (TOKENS, HEADS * HD), jnp.float32), -8.0, 8.0)
    return base.astype(jnp.bfloat16)


def draw_block_mask(key, part):
    key = jax.random.fold_in(key, 5)
    frames = QBLOCKS // BLK_F
    frame_ids = jnp.arange(frames, dtype=jnp.int32)
    within = jnp.arange(BLK_F, dtype=jnp.int32)
    own_blocks = jnp.broadcast_to(frame_ids[:, None, None] * BLK_F + within[None, None, :], (frames, BLK_F, BLK_F))
    columns = [own_blocks]
    for octave in range(LEVELS):
        extent = max(2, BLK_F >> octave)
        for direction in range(2):
            subkey = jax.random.fold_in(jax.random.fold_in(key, octave + 1), direction)
            ranks = jax.random.randint(subkey, (frames, BLK_F), 0, 1 << 20) * BLK_F + within[None, :]
            order = jnp.argsort(ranks, axis=1).astype(jnp.int32)
            start = jax.random.randint(jax.random.fold_in(subkey, 7), (frames,), 0, extent)
            partner = frame_ids + (2 * direction - 1) * 2 ** octave
            inside = (partner >= 0) & (partner < frames)
            spots = (start[:, None, None] + 2 * within[None, :, None] + jnp.arange(2, dtype=jnp.int32)[None, None, :]) % extent
            local_block = jnp.take_along_axis(order, spots.reshape(frames, 2 * BLK_F), axis=1).reshape(frames, BLK_F, 2)
            named = jnp.where(inside[:, None, None], partner[:, None, None] * BLK_F + local_block, -1)
            columns.append(named.astype(jnp.int32))
    return jnp.concatenate(columns, axis=2).reshape(QBLOCKS, SLOTS).astype(jnp.int32)


def levels(rng, shape, shards, least, top_value):
    loudness, own = 1.0, jax.random.fold_in(rng, 6)
    for position, blocks in shards:
        heights = jnp.exp(jax.random.uniform(jax.random.fold_in(own, position), (blocks,), jnp.float32, least / len(shards), top_value / len(shards)))
        loudness = loudness * jnp.repeat(heights, shape[position] // blocks).reshape([-1 if axis == position else 1 for axis in range(len(shape))])
    return loudness


def bell_draw(own_key, shape, scale, reach, pieces=(), held_as=jnp.bfloat16):
    factor_of = levels(own_key, shape, pieces, -0.22, 0.18) if pieces else 1.0
    result = jax.random.normal(own_key, shape, jnp.float32) * scale * factor_of
    return jnp.minimum(jnp.maximum(result, -reach), reach).astype(held_as)


def setup_inputs(seed: int = 0) -> dict:
    streams_of = jax.random.split(jax.random.key(seed), 6)
    return {
        "queries": draw_queries(jax.random.fold_in(streams_of[5], 71), 0),
        "key_rows": draw_key_rows(jax.random.fold_in(streams_of[5], 71), 0),
        "value_rows": bell_draw(streams_of[2], (TOKENS, HEADS * HD), 1.0, 6.0, ((0, 64), (1, 2))),
        "block_mask": draw_block_mask(jax.random.fold_in(streams_of[5], 71), 0),
        "out_weight": bell_draw(streams_of[4], (HEADS * HD, D), (HEADS * HD) ** -0.5, 0.109375, ((0, 2),)),
    }


def reference(queries, key_rows, value_rows, block_mask, out_weight):
    key_blocks = key_rows.reshape(QBLOCKS, BLK, HEADS, HD)
    value_blocks = value_rows.reshape(QBLOCKS, BLK, HEADS, HD)
    query_blocks = queries.reshape(QBLOCKS, BLK, HEADS, HD)
    inv_root = 1.0 / math.sqrt(HD)

    def attend_block(operands):
        qblock, slot_row = operands
        slot_ok = slot_row >= 0
        safe_index = jnp.where(slot_ok, slot_row, 0).astype(jnp.int32)
        key_part = key_blocks[safe_index].astype(jnp.float32)
        value_part = value_blocks[safe_index].astype(jnp.float32)
        scores = jnp.einsum('qhd,sbhd->hqsb', qblock.astype(jnp.float32), key_part) * inv_root
        scores = jnp.where(slot_ok[None, None, :, None], scores, -jnp.inf)
        peak = lax.optimization_barrier(jnp.max(scores, axis=(2, 3), keepdims=True))
        raised = jnp.exp(scores - peak)
        total = lax.optimization_barrier(jnp.sum(raised, axis=(2, 3), keepdims=True))
        weights = (raised / total).astype(jnp.bfloat16)
        mixed = jnp.einsum('hqsb,sbhd->qhd', weights.astype(jnp.float32), value_part)
        return mixed.astype(jnp.bfloat16).reshape(BLK, HEADS * HD)
    heads_out = lax.map(attend_block, (query_blocks, block_mask)).reshape(TOKENS, HEADS * HD)
    return jnp.dot(heads_out, out_weight, preferred_element_type=jnp.float32).astype(jnp.bfloat16)
```

```python
import functools
import math

import jax
import jax.numpy as jnp
from jax import lax
from jax.experimental import pallas as pl
from jax.experimental.pallas import tpu as pltpu
from jax.sharding import PartitionSpec as P

HD = 128
BLK = 64
BF = 8
G = 4
SLOTS = 32
GB = G * BF
LOW = -1e30
C = math.log2(math.e) / math.sqrt(HD)
VMEM = 56 * 1024 * 1024
EXT = 26


def line_pairs(frames, shift):
    return [(f, f // G * G + (f + shift) % G) for f in range(frames)]


def group_pairs(frames, distance):
    return [(f, f + G * distance) for f in range(frames) if 0 <= f + G * distance < frames]


def swap_pairs(frames):
    return [(f, f ^ (frames // 2)) for f in range(frames)]


def softmax_part(q, k_ref, v_ref, bias_ref, first_block, blocks, start):
    keys = k_ref.shape[0]
    s = lax.dot_general(q, k_ref[...], (((1,), (1,)), ((), ())), preferred_element_type=jnp.float32)
    s = s.reshape(blocks, BLK, keys) * C
    s = s + bias_ref[pl.ds(first_block, blocks)]
    s = s.reshape(blocks * BLK, keys)
    peak = jnp.max(s, axis=1, keepdims=True)
    if start is not None:
        peak = jnp.maximum(peak, start)
    raised = jnp.exp2(s - peak)
    total = jnp.sum(raised, axis=1, keepdims=True)
    mixed = jnp.dot(raised.astype(jnp.bfloat16), v_ref[...], preferred_element_type=jnp.float32)
    return peak, total, mixed


QT = 4


def inner_kernel(q_ref, k_ref, v_ref, bias_ref, acc_ref, peak_ref, total_ref):
    rows = QT * BLK

    def step(t, _):
        at = pl.ds(pl.multiple_of(t * rows, rows), rows)
        peak, total, mixed = softmax_part(q_ref[at, :], k_ref, v_ref, bias_ref, t * QT, QT, None)
        acc_ref[at, :] = mixed
        peak_ref[at, :] = jnp.broadcast_to(peak, (rows, HD))
        total_ref[at, :] = jnp.broadcast_to(total, (rows, HD))
        return 0

    lax.fori_loop(0, q_ref.shape[0] // rows, step, 0)


def inner(q, kv, bias):
    tokens, features = q.shape
    heads = features // HD
    column = pl.BlockSpec((tokens, HD), lambda h: (0, h))
    shape = jax.ShapeDtypeStruct((tokens, features), jnp.float32)
    return pl.pallas_call(
        inner_kernel,
        grid=(heads,),
        in_specs=[
            column,
            column,
            pl.BlockSpec((tokens, HD), lambda h: (0, heads + h)),
            pl.BlockSpec(bias.shape, lambda h: (0, 0, 0)),
        ],
        out_specs=[column, column, column],
        out_shape=[shape, shape, shape],
        compiler_params=pltpu.CompilerParams(vmem_limit_bytes=VMEM),
        cost_estimate=pl.CostEstimate(
            flops=4 * tokens * tokens * features, bytes_accessed=16 * tokens * features, transcendentals=tokens * tokens * heads
        ),
    )(q, kv, kv, bias)


def outer_kernel(counts, table, q_ref, bias_ref, acc_ref, peak_ref, total_ref, *rest):
    pieces = rest[: len(counts)]
    out_ref, held, k_all, v_all, sems = rest[len(counts) :]
    heads = held.shape[2] // HD // 2
    head, slot = pl.program_id(0), pl.program_id(1)
    rows = QT * BLK

    @pl.when((head == 0) & (slot == 0))
    def _():
        copies = []
        begin = 0
        for i, (count, piece) in enumerate(zip(counts, pieces)):
            copies.append(pltpu.make_async_copy(piece, held.at[pl.ds(begin, count)], sems.at[i]))
            begin += count
        for copy in copies:
            copy.start()
        for copy in copies:
            copy.wait()

    for h in range(heads):

        @pl.when(head == h)
        def _():
            for e in range(EXT):
                block = table[slot * EXT + e]
                k_all[e * BLK : (e + 1) * BLK, :] = held[block, :, h * HD : (h + 1) * HD]
                v_all[e * BLK : (e + 1) * BLK, :] = held[block, :, (heads + h) * HD : (heads + h + 1) * HD]

    def step(t, _):
        at = pl.ds(pl.multiple_of(t * rows, rows), rows)
        before = peak_ref[at, :1]
        peak, total, mixed = softmax_part(q_ref[at, :], k_all, v_all, bias_ref, t * QT, QT, before)
        keep = jnp.exp2(before - peak)
        total = total + total_ref[at, :1] * keep
        out_ref[at, :] = ((mixed + acc_ref[at, :] * keep) / total).astype(out_ref.dtype)
        return 0

    lax.fori_loop(0, q_ref.shape[0] // rows, step, 0)


def outer(table, q, bias, partial, pieces):
    tokens, features = q.shape
    heads = features // HD
    rows = tokens // G
    counts = tuple(piece.shape[0] for piece in pieces)
    spec = pl.BlockSpec((rows, HD), lambda h, s, *_: (s, h))
    return pl.pallas_call(
        functools.partial(outer_kernel, counts),
        grid_spec=pltpu.PrefetchScalarGridSpec(
            num_scalar_prefetch=1,
            grid=(heads, G),
            in_specs=[
                spec,
                pl.BlockSpec((BF, 1, EXT * BLK), lambda h, s, *_: (s, 0, 0)),
                spec,
                spec,
                spec,
            ]
            + [pl.BlockSpec(memory_space=pl.ANY)] * len(pieces),
            out_specs=spec,
            scratch_shapes=[
                pltpu.VMEM((sum(counts), BLK, 2 * features), jnp.bfloat16),
                pltpu.VMEM((EXT * BLK, HD), jnp.bfloat16),
                pltpu.VMEM((EXT * BLK, HD), jnp.bfloat16),
                pltpu.SemaphoreType.DMA((len(counts),)),
            ],
        ),
        out_shape=jax.ShapeDtypeStruct((tokens, features), jnp.bfloat16),
        compiler_params=pltpu.CompilerParams(vmem_limit_bytes=VMEM),
        cost_estimate=pl.CostEstimate(
            flops=4 * tokens * EXT * BLK * features, bytes_accessed=16 * tokens * features, transcendentals=tokens * EXT * BLK * heads
        ),
    )(table.reshape(-1), q, bias, *partial, *pieces)


def named(mask, frame, y):
    return lax.dynamic_index_in_dim(mask, (y - frame) % G, 0, keepdims=False)


def distinct(entries, first, count):
    within = jnp.arange(BF, dtype=jnp.int32)
    present = jnp.any(entries.reshape(-1)[:, None] == (first + within)[None, :], axis=0)
    rank = jnp.cumsum(present.astype(jnp.int32))
    hit = present[None, :] & (rank[None, :] == 1 + jnp.arange(count, dtype=jnp.int32)[:, None])
    return first + jnp.sum(jnp.where(hit, within[None, :], 0), axis=1)


def requests(mask, a, y):
    within = jnp.arange(BF, dtype=jnp.int32)
    frames = [named(mask, i, y) for i in range(G)]
    below, above = (a - 1) * GB, (a + 1) * GB
    m1 = jnp.concatenate(
        [
            below + 3 * BF + within,
            distinct(frames[0][:, 12:14], below + 2 * BF, 4),
            frames[2][0, 16:18],
            frames[1][0, 16:18],
            frames[0][0, 16:18],
        ]
    )
    p1 = jnp.concatenate(
        [
            above + within,
            distinct(frames[3][:, 14:16], above + BF, 4),
            frames[1][0, 18:20],
            frames[2][0, 18:20],
            frames[3][0, 18:20],
        ]
    )
    far = [mask[:, 0, c : c + 2].reshape(-1) for c in (20, 22, 24, 26)]
    swap = jnp.maximum(mask[:, 0, 28:30], mask[:, 0, 30:32]).reshape(-1)
    return [m1, p1, *far, swap]


def on_device(queries, key_rows, value_rows, block_mask, out_weight):
    n = lax.axis_size("frame")
    position = lax.axis_index("frame")
    y, a = position % G, position // G
    tokens, features = queries.shape
    share = features // G

    def line(value, shift):
        return lax.ppermute(value, "frame", line_pairs(n, shift))

    def reach(distance):
        return swap_pairs(n) if distance == 8 else group_pairs(n, distance)

    def chunk(x, shift):
        return lax.dynamic_slice_in_dim(x, (y + shift) % G * share, share, 1)

    kv = [jnp.concatenate([chunk(key_rows, s), chunk(value_rows, s)], axis=1) for s in range(G)]
    kv = jnp.stack([kv[0]] + [line(kv[s], s) for s in (1, 2, 3)])
    q = jnp.concatenate([chunk(queries, 0)] + [line(chunk(queries, s), s) for s in (1, 2, 3)], axis=0)
    blocks = kv.reshape(GB, BLK, 2 * share)

    mask = jnp.stack([block_mask] + [line(block_mask, s) for s in (1, 2, 3)])
    wanted = requests(mask, a, y)
    sizes = [w.shape[0] for w in wanted]
    distances = (-1, 1, -2, 2, -4, 4, 8)
    pieces = []
    for w, d in zip(wanted, distances):
        asked = lax.ppermute(w, "frame", reach(d))
        local = jnp.clip(asked - a * GB, 0, GB - 1)
        index = (y - local // BF) % G * BF + local % BF
        back = 8 if d == 8 else -d
        pieces.append(lax.ppermute(blocks[index], "frame", reach(back)))

    rows = mask.reshape(GB, SLOTS)
    slots = jnp.arange(G, dtype=jnp.int32)
    frame_of = (y - slots) % G
    ids = (a * GB + frame_of[:, None] * BF + jnp.arange(BF, dtype=jnp.int32)[None, :]).reshape(-1)
    hit = jnp.any(rows[:, :, None] == ids[None, None, :], axis=1)
    bias_in = jnp.repeat(jnp.where(hit, 0.0, LOW), BLK, axis=1)[:, None, :]

    starts = [sum(sizes[:i]) for i in range(len(sizes))]
    m1, p1 = starts[0], starts[1]
    flat = jnp.concatenate(wanted)
    three = mask[(y - 3) % G, 0, 16:18] - ((a - 1) * GB + 3 * BF)
    zero = mask[y % G, 0, 18:20] - (a + 1) * GB
    within = jnp.arange(BF, dtype=jnp.int32)
    none = jnp.full((4,), -1, jnp.int32)
    four = jnp.arange(4, dtype=jnp.int32)
    two = jnp.arange(2, dtype=jnp.int32)
    tables = jnp.stack(
        [
            jnp.concatenate([m1 + within, m1 + 8 + four, m1 + 16 + two, p1 + jnp.clip(zero, 0, BF - 1)]),
            jnp.concatenate([m1 + within, none, m1 + 14 + two, p1 + 12 + two]),
            jnp.concatenate([p1 + within, none, m1 + 12 + two, p1 + 14 + two]),
            jnp.concatenate([p1 + within, p1 + 8 + four, m1 + jnp.clip(three, 0, BF - 1), p1 + 16 + two]),
        ]
    )[frame_of]
    far = jnp.concatenate(
        [start + 2 * slots[:, None] + two[None, :] for start in starts[2:]], axis=1
    )
    table = jnp.concatenate([tables, far], axis=1)
    held = jnp.where(table >= 0, flat[jnp.maximum(table, 0)], -1)
    hit = (rows.reshape(G, BF, SLOTS, 1) == held[:, None, None, :]) & (held >= 0)[:, None, None, :]
    hit = jnp.any(hit, axis=2).reshape(GB, EXT)
    bias_out = jnp.repeat(jnp.where(hit, 0.0, LOW), BLK, axis=1)[:, None, :]

    partial = inner(q, kv.reshape(G * tokens, 2 * share), bias_in)
    heads_out = outer(jnp.maximum(table, 0), q, bias_out, partial, pieces).reshape(G, tokens, share)

    mixed = jnp.concatenate([heads_out[0]] + [line(heads_out[G - s], s) for s in (1, 2, 3)], axis=1)
    weight = jnp.concatenate(
        [lax.dynamic_slice_in_dim(out_weight, (y - s) % G * share, share, 0) for s in range(G)], axis=0
    )
    half = tokens // 2
    core = lax.axis_index("head")
    theirs = lax.dynamic_slice_in_dim(mixed, (1 - core) * half, half, 0)
    ours = lax.dynamic_slice_in_dim(mixed, core * half, half, 0)
    sent = jnp.dot(theirs, weight, preferred_element_type=jnp.float32).astype(jnp.bfloat16)
    other = lax.ppermute(sent, "head", [(0, 1), (1, 0)])
    kept = jnp.dot(ours, weight, preferred_element_type=jnp.float32)
    return (kept + other.astype(jnp.float32)).astype(jnp.bfloat16)


def solution(mesh):
    in_specs = (
        P("frame", "head"),
        P("frame", "head"),
        P("frame", "head"),
        P("frame", None),
        P("head", None),
    )
    out_specs = P(("frame", "head"), None)
    return jax.shard_map(
        on_device, mesh=mesh, in_specs=in_specs, out_specs=out_specs, check_vma=False
    )
```

```python
import functools
import math

import jax
import jax.numpy as jnp
from jax import lax
from jax.experimental import pallas as pl
from jax.experimental.pallas import tpu as pltpu
from jax.sharding import PartitionSpec as P

HD = 128
BLK = 64
BF = 8
G = 4
SLOTS = 32
GB = G * BF
FT = BF * BLK
LOW = -1e30
C = math.log2(math.e) / math.sqrt(HD)
VMEM = 56 * 1024 * 1024


STAGES = ((0, 1), (1, 2))

PIECES = ((-1, 18), (1, 18), (-2, 8), (2, 8), (-4, 8), (4, 8), (8, 8))
FAR = ((2, 20), (3, 22), (4, 24), (5, 26))
STARTS = [sum(count for _, count in PIECES[:i]) for i in range(len(PIECES) + 1)]


def span(piece, first, count):
    return [(piece, first + j) for j in range(count)]


NEAR = (
    span(0, 0, 12) + span(0, 16, 2) + [(1, "zero0"), (1, "zero1")],
    span(0, 0, 8) + span(0, 14, 2) + span(1, 12, 2),
    span(1, 0, 8) + span(0, 12, 2) + span(1, 14, 2),
    span(1, 0, 12) + [(0, "three0"), (0, "three1")] + span(1, 16, 2),
)
READS = [near + [(2 + n, 2 * i + r) for n in range(5) for r in range(2)] for i, near in enumerate(NEAR)]
EXT = max(len(reads) for reads in READS)
NAMES = ("zero0", "zero1", "three0", "three1")


def smem():
    return pl.BlockSpec(memory_space=pltpu.SMEM)


def hbm():
    return pl.BlockSpec(memory_space=pl.ANY)


def line_pairs(frames, shift):
    return [(f, f // G * G + (f + shift) % G) for f in range(frames)]


def group_pairs(frames, distance):
    return [(f, f + G * distance) for f in range(frames) if 0 <= f + G * distance < frames]


def swap_pairs(frames):
    return [(f, f ^ (frames // 2)) for f in range(frames)]


def plan_kernel(groups, where, masks, send, numbers, ids, own):
    a = where[1]

    def wanted(piece, group, put):
        def entry(frame, row, column):
            return masks[((group * G + frame) * BF + row) * SLOTS + column]

        below, above = (group - 1) * GB, (group + 1) * GB

        def pair(at, frame, column):
            for r in range(2):
                put(at + r, entry(frame, 0, column + r))

        def distinct(frame, column, first):
            bits = jnp.int32(0)
            for row in range(BF):
                for r in range(2):
                    offset = entry(frame, row, column + r) - first
                    inside = (offset >= 0) & (offset < BF)
                    bits = bits | jnp.where(inside, jnp.int32(1) << jnp.clip(offset, 0, BF - 1), 0)
            for c in range(4):
                put(8 + c, first)
            count = jnp.int32(0)
            for j in range(BF):
                here = (bits >> j) & 1

                @pl.when((here == 1) & (count < 4))
                def _(count=count, j=j):
                    put(8 + count, first + j)

                count = count + here

        if piece == 0:
            for j in range(BF):
                put(j, below + 3 * BF + j)
            distinct(0, 12, below + 2 * BF)
            for n, frame in enumerate((2, 1, 0)):
                pair(12 + 2 * n, frame, 16)
        elif piece == 1:
            for j in range(BF):
                put(j, above + j)
            distinct(3, 14, above + BF)
            for n, frame in enumerate((1, 2, 3)):
                pair(12 + 2 * n, frame, 18)
        elif piece < 6:
            column = dict(FAR)[piece]
            for frame in range(G):
                pair(2 * frame, frame, column)
        else:
            for frame in range(G):
                for r in range(2):
                    put(2 * frame + r, jnp.maximum(entry(frame, 0, 28 + r), entry(frame, 0, 30 + r)))

    for p, (distance, _) in enumerate(PIECES):
        other = jnp.where(a < groups // 2, a + groups // 2, a - groups // 2) if distance == 8 else a - distance
        other = jnp.clip(other, 0, groups - 1)

        def put_send(at, block, p=p):
            send[STARTS[p] + at] = jnp.clip(block - a * GB, 0, GB - 1)

        def put_own(at, block, p=p):
            own[STARTS[p] + at] = block

        wanted(p, other, put_send)
        wanted(p, a, put_own)
    for r in range(2):
        zero = masks[(a * G * BF) * SLOTS + 18 + r]
        three = masks[((a * G + 3) * BF) * SLOTS + 16 + r]
        numbers[r] = jnp.clip(zero - (a + 1) * GB, 0, BF - 1)
        numbers[2 + r] = jnp.clip(three - (a - 1) * GB - 3 * BF, 0, BF - 1)
        ids[14 + r] = zero
        ids[3 * EXT + 12 + r] = three
    for frame, reads in enumerate(READS):
        for e in range(EXT):
            if e >= len(reads):
                ids[frame * EXT + e] = -1
            elif reads[e][1] not in NAMES:
                ids[frame * EXT + e] = own[STARTS[reads[e][0]] + reads[e][1]]


def plan(groups, where, masks):
    shapes = [jax.ShapeDtypeStruct((count,), jnp.int32) for count in (STARTS[-1], len(NAMES), G * EXT)]
    return pl.pallas_call(
        functools.partial(plan_kernel, groups),
        in_specs=[smem()] * 2,
        out_specs=[smem()] * 3,
        out_shape=shapes,
        scratch_shapes=[pltpu.SMEM((STARTS[-1],), jnp.int32)],
    )(where, masks)


def split_kernel(takes, where, *refs):
    n = len(takes)
    sources, outs, sems = refs[:n], refs[n : n + G], refs[-1]
    y = where[0]
    share = sources[0].shape[1] // G
    for s in range(G):
        to = 0
        for source, (first, heads) in zip(sources, takes):
            column = pl.multiple_of(lax.rem(y + s, G) * share + first * HD, HD)
            pltpu.make_async_copy(
                source.at[:, pl.ds(column, heads * HD)], outs[s].at[:, pl.ds(to, heads * HD)], sems.at[s]
            ).start()
            to += heads * HD
    for s in range(G):
        pltpu.make_async_copy(outs[s], outs[s], sems.at[s]).wait()


def split(where, sources, takes):
    width = sum(heads for _, heads in takes) * HD
    shape = jax.ShapeDtypeStruct((sources[0].shape[0], width), sources[0].dtype)
    return pl.pallas_call(
        functools.partial(split_kernel, takes),
        in_specs=[smem()] + [pl.BlockSpec(memory_space=pltpu.VMEM)] * len(sources),
        out_specs=[hbm()] * G,
        out_shape=[shape] * G,
        scratch_shapes=[pltpu.SemaphoreType.DMA((G,))],
        compiler_params=pltpu.CompilerParams(vmem_limit_bytes=VMEM),
    )(where, *sources)


def pack_kernel(where, send, *refs):
    parts, outs = refs[:G], refs[G : G + len(PIECES)]
    held, ins, sems = refs[G + len(PIECES) :]
    y = where[0]
    width = held.shape[1]
    loads = []
    for s, part in enumerate(parts):
        row = pl.multiple_of(lax.rem(y - s + G, G) * FT, FT)
        loads.append(pltpu.make_async_copy(part.at[:, pl.ds(0, width)], held.at[pl.ds(row, FT)], ins.at[s]))
    for load in loads:
        load.start()
    for load in loads:
        load.wait()
    for p, (_, count) in enumerate(PIECES):
        for j in range(count):
            row = pl.multiple_of(send[STARTS[p] + j] * BLK, BLK)
            pltpu.make_async_copy(held.at[pl.ds(row, BLK)], outs[p].at[j], sems.at[p]).start()
    for p in range(len(PIECES)):
        pltpu.make_async_copy(outs[p], outs[p], sems.at[p]).wait()


def pack(where, send, parts, heads):
    width = 2 * heads * HD
    dtype = parts[0].dtype
    return pl.pallas_call(
        pack_kernel,
        in_specs=[smem()] * 2 + [hbm()] * G,
        out_specs=[hbm()] * len(PIECES),
        out_shape=[jax.ShapeDtypeStruct((count, BLK, width), dtype) for _, count in PIECES],
        scratch_shapes=[
            pltpu.VMEM((G * FT, width), dtype),
            pltpu.SemaphoreType.DMA((G,)),
            pltpu.SemaphoreType.DMA((len(PIECES),)),
        ],
        compiler_params=pltpu.CompilerParams(vmem_limit_bytes=VMEM),
    )(where, send, *parts)


def marks(first):
    row = lax.broadcasted_iota(jnp.int32, (FT, HD), 0) // BLK + first
    return jnp.where(row == lax.broadcasted_iota(jnp.int32, (FT, HD), 1), 1.0, 0.0).astype(jnp.bfloat16)


def inner_kernel(where, *refs):
    q_parts, k_parts, v_parts = refs[:G], refs[G : 2 * G], refs[2 * G : 3 * G]
    bias_ref, acc_ref, peak_ref, total_ref, q_all, k_all, v_all = refs[3 * G :]
    y = where[0]

    @pl.when(pl.program_id(0) == 0)
    def _():
        k_all[:, HD:] = bias_ref[...]
        v_all[:, HD:] = jnp.ones((G * FT, HD), jnp.bfloat16)
        for i in range(G):
            q_all[i * FT : (i + 1) * FT, HD:] = marks(i * BF)

    for s in range(G):
        at = pl.ds(pl.multiple_of(lax.rem(y - s + G, G) * FT, FT), FT)
        q_all[at, :HD] = q_parts[s][...]
        k_all[at, :HD] = k_parts[s][...]
        v_all[at, :HD] = v_parts[s][...]
    for i in range(G):
        at = slice(i * FT, (i + 1) * FT)
        keys = slice(max(0, i - 2) * FT, min(G, i + 3) * FT)
        s = lax.dot_general(
            q_all[at, :], k_all[keys, :], (((1,), (1,)), ((), ())), preferred_element_type=jnp.float32
        )
        peak = jnp.max(s, axis=1, keepdims=True)
        raised = jnp.exp2(s * C - peak * C)
        both = jnp.dot(raised.astype(jnp.bfloat16), v_all[keys, :], preferred_element_type=jnp.float32)
        acc_ref[at, :] = both[:, :HD]
        total_ref[at, :] = both[:, HD:]
        peak_ref[at, :] = jnp.broadcast_to(peak, (FT, HD))


def inner(where, parts, heads, bias):
    tokens = G * FT
    column = pl.BlockSpec((tokens, HD), lambda h: (0, h))
    shape = jax.ShapeDtypeStruct((tokens, heads * HD), jnp.float32)

    def part(begin):
        return [pl.BlockSpec((FT, HD), lambda h: (0, begin + h))] * G

    return pl.pallas_call(
        inner_kernel,
        grid=(heads,),
        in_specs=[smem(), *part(2 * heads), *part(0), *part(heads), pl.BlockSpec(bias.shape, lambda h: (0, 0))],
        out_specs=[column, column, column],
        out_shape=[shape, shape, shape],
        scratch_shapes=[pltpu.VMEM((tokens, 2 * HD), jnp.bfloat16)] * 3,
        compiler_params=pltpu.CompilerParams(vmem_limit_bytes=VMEM),
        cost_estimate=pl.CostEstimate(
            flops=8 * tokens * tokens * heads * HD,
            bytes_accessed=16 * tokens * heads * HD,
            transcendentals=tokens * tokens * heads,
        ),
    )(where, *parts, *parts, *parts, bias)


def outer_kernel(where, numbers, *refs):
    n = len(PIECES)
    q_parts, k_pieces, v_pieces = refs[:G], refs[G : G + n], refs[G + n : G + 2 * n]
    bias_ref, acc_ref, peak_ref, total_ref, *outs = refs[G + 2 * n : 2 * G + 2 * n + 4]
    out_all, q_all, k_all, v_all = refs[2 * G + 2 * n + 4 :]
    y = where[0]

    @pl.when(pl.program_id(0) == 0)
    def _():
        k_all[:, :, HD:] = bias_ref[...]
        v_all[:, :, HD:] = jnp.ones((G, EXT * BLK, HD), jnp.bfloat16)
        for i in range(G):
            q_all[i * FT : (i + 1) * FT, HD:] = marks(0)

    for s in range(G):
        at = pl.ds(pl.multiple_of(lax.rem(y - s + G, G) * FT, FT), FT)
        q_all[at, :HD] = q_parts[s][...]
    for i, reads in enumerate(READS):
        for e, (piece, block) in enumerate(reads):
            if block in NAMES:
                block = numbers[NAMES.index(block)]
            k_all[i, e * BLK : (e + 1) * BLK, :HD] = k_pieces[piece][block]
            v_all[i, e * BLK : (e + 1) * BLK, :HD] = v_pieces[piece][block]
    for i, reads in enumerate(READS):
        at = slice(i * FT, (i + 1) * FT)
        keys = slice(0, len(reads) * BLK)
        s = lax.dot_general(
            q_all[at, :], k_all[i, keys, :], (((1,), (1,)), ((), ())), preferred_element_type=jnp.float32
        )
        before = peak_ref[at, :1]
        peak = jnp.maximum(jnp.max(s, axis=1, keepdims=True), before)
        raised = jnp.exp2(s * C - peak * C)
        both = jnp.dot(raised.astype(jnp.bfloat16), v_all[i, keys, :], preferred_element_type=jnp.float32)
        keep = jnp.exp2((before - peak) * C)
        total = both[:, HD:] + total_ref[at, :] * keep
        row = pl.multiple_of(lax.rem(y - i + G, G) * FT, FT)
        out_all[pl.ds(row, FT), :] = ((both[:, :HD] + acc_ref[at, :] * keep) / total).astype(out_all.dtype)
    for s in range(G):
        outs[s][...] = out_all[s * FT : (s + 1) * FT, :]


def outer(where, numbers, parts, heads, bias, partial, pieces):
    tokens = G * FT
    column = pl.BlockSpec((tokens, HD), lambda h: (0, h))

    def piece(kind):
        return [pl.BlockSpec((count, BLK, HD), lambda h: (0, 0, kind * heads + h)) for _, count in PIECES]

    return pl.pallas_call(
        outer_kernel,
        grid=(heads,),
        in_specs=[smem(), smem()]
        + [pl.BlockSpec((FT, HD), lambda h: (0, 2 * heads + h))] * G
        + piece(0)
        + piece(1)
        + [pl.BlockSpec(bias.shape, lambda h: (0, 0, 0)), column, column, column],
        out_specs=[pl.BlockSpec((FT, HD), lambda h: (0, h))] * G,
        out_shape=[jax.ShapeDtypeStruct((FT, heads * HD), jnp.bfloat16)] * G,
        scratch_shapes=[
            pltpu.VMEM((tokens, HD), jnp.bfloat16),
            pltpu.VMEM((tokens, 2 * HD), jnp.bfloat16),
            pltpu.VMEM((G, EXT * BLK, 2 * HD), jnp.bfloat16),
            pltpu.VMEM((G, EXT * BLK, 2 * HD), jnp.bfloat16),
        ],
        compiler_params=pltpu.CompilerParams(vmem_limit_bytes=VMEM),
        cost_estimate=pl.CostEstimate(
            flops=8 * tokens * EXT * BLK * heads * HD,
            bytes_accessed=16 * tokens * heads * HD,
            transcendentals=tokens * EXT * BLK * heads,
        ),
    )(where, numbers, *parts, *pieces, *pieces, bias, *partial)


def project_kernel(where, *refs):
    n = G * len(STAGES)
    parts, weight, sent_ref, kept_ref, mixed, sems = refs[:n], refs[n], *refs[n + 1 :]
    y, core = where[0], where[2]
    half = sent_ref.shape[0]
    share = mixed.shape[1] // G

    @pl.when(pl.program_id(0) == 0)
    def _():
        loads = []
        for i, (head, heads) in enumerate(STAGES):
            for s in range(G):
                column = pl.multiple_of(lax.rem(y - s + G, G) * share + head * HD, HD)
                for k, begin in enumerate((1 - core, core)):
                    loads.append(
                        pltpu.make_async_copy(
                            parts[i * G + s].at[pl.ds(pl.multiple_of(begin * half, half), half)],
                            mixed.at[pl.ds(k * half, half), pl.ds(column, heads * HD)],
                            sems.at[2 * (i * G + s) + k],
                        )
                    )
        for load in loads:
            load.start()
        for load in loads:
            load.wait()

    both = jnp.dot(mixed[...], weight[...], preferred_element_type=jnp.float32)
    sent_ref[...] = both[:half].astype(sent_ref.dtype)
    kept_ref[...] = both[half:]


def project(where, parts, weight, begin, end):
    rows, tile = parts[0].shape[0], 512
    depth = weight.shape[0]
    column = pl.BlockSpec((rows // 2, tile), lambda j: (0, j))
    return pl.pallas_call(
        project_kernel,
        grid=((end - begin) // tile,),
        in_specs=[smem()]
        + [hbm()] * len(parts)
        + [pl.BlockSpec((depth, tile), lambda j: (0, begin // tile + j))],
        out_specs=[column, column],
        out_shape=[
            jax.ShapeDtypeStruct((rows // 2, end - begin), jnp.bfloat16),
            jax.ShapeDtypeStruct((rows // 2, end - begin), jnp.float32),
        ],
        scratch_shapes=[pltpu.VMEM((rows, depth), jnp.bfloat16), pltpu.SemaphoreType.DMA((2 * len(parts),))],
        compiler_params=pltpu.CompilerParams(vmem_limit_bytes=VMEM),
        cost_estimate=pl.CostEstimate(
            flops=2 * rows * depth * (end - begin), bytes_accessed=2 * depth * (end - begin), transcendentals=0
        ),
    )(where, *parts, weight)


def after(values, *others):
    flat, tree = jax.tree.flatten(values)
    out = lax.optimization_barrier(tuple(flat) + tuple(jax.tree.leaves(others)))
    return jax.tree.unflatten(tree, out[: len(flat)])


def on_device(queries, key_rows, value_rows, block_mask, out_weight):
    n = lax.axis_size("frame")
    position = lax.axis_index("frame")
    y, a = position % G, position // G
    where = jnp.stack([y, a, lax.axis_index("head")]).astype(jnp.int32)

    def line(value, shift):
        return lax.ppermute(value, "frame", line_pairs(n, shift))

    def spread(parts):
        return [parts[0]] + [line(parts[s], s) for s in (1, 2, 3)]

    def travel(parts, which):
        pairs = {p: swap_pairs(n) if PIECES[p][0] == 8 else group_pairs(n, -PIECES[p][0]) for p in which}
        return {p: lax.ppermute(parts[p], "frame", pairs[p]) for p in which}

    masks = lax.all_to_all(
        jnp.broadcast_to(block_mask[None], (n, BF, SLOTS)), "frame", 0, 0, tiled=True
    )
    chunks = split(where, (key_rows, value_rows, queries), (STAGES[0],) * 3)
    later = split(where, after((key_rows, value_rows, queries), chunks), (STAGES[1],) * 3)
    parts = [spread(chunks), None]
    parts[1] = spread(after(later, parts[0]))
    send, numbers, ids = plan(n // G, where, after(masks.reshape(-1), later))

    rows = lax.dynamic_slice_in_dim(masks, a * G, G, 0)
    inside = a * GB + jnp.arange(GB, dtype=jnp.int32)
    hit = jnp.any(rows.reshape(1, GB, SLOTS) == inside[:, None, None], axis=2)
    bias = jnp.pad(jnp.where(hit, 0.0, LOW).astype(jnp.bfloat16), ((0, 0), (0, HD - GB)))
    bias_in = jnp.repeat(bias, BLK, axis=0)
    held = ids.reshape(G, EXT, 1, 1)
    hit = jnp.any((rows.reshape(G, 1, BF, SLOTS) == held) & (held >= 0), axis=3)
    bias = jnp.pad(jnp.where(hit, 0.0, LOW).astype(jnp.bfloat16), ((0, 0), (0, 0), (0, HD - BF)))
    bias_out = jnp.repeat(bias, BLK, axis=1)

    def within(i, *others):
        return inner(where, after(parts[i], *others), STAGES[i][1], bias_in)

    def beyond(i, partial):
        pieces = [got[i][p] for p in range(len(PIECES))]
        return outer(where, numbers, parts[i], STAGES[i][1], bias_out, partial, pieces)

    got = [{}, {}]
    first = pack(where, send, parts[0], STAGES[0][1])
    got[0].update(travel(first, (0, 1)))
    partial0 = within(0, first)
    got[0].update(travel(after(first, got[0], partial0), (2, 3)))
    second = pack(where, send, parts[1], STAGES[1][1])
    got[1].update(travel(second, (0, 1)))
    got[0].update(travel(after(first, got[0][2], got[0][3]), (4, 5, 6)))
    partial1 = within(1, second)
    got[1].update(travel(after(second, partial1, got[1]), (2, 3)))
    got[1].update(travel(after(second, partial1, got[0]), (4, 5, 6)))

    outs = beyond(0, after(partial0, partial1))
    mixed = spread([outs[(G - s) % G] for s in range(G)])
    outs = beyond(1, partial1)
    mixed += spread([outs[(G - s) % G] for s in range(G)])

    columns = out_weight.shape[1]
    outs = []
    for begin in (0, columns // 2):
        sent, kept = project(where, mixed, out_weight, begin, begin + columns // 2)
        outs.append((kept, lax.ppermute(sent, "head", [(0, 1), (1, 0)])))
    return jnp.concatenate([(k + o.astype(jnp.float32)).astype(jnp.bfloat16) for k, o in outs], axis=1)


def solution(mesh):
    in_specs = (
        P("frame", "head"),
        P("frame", "head"),
        P("frame", "head"),
        P("frame", None),
        P("head", None),
    )
    out_specs = P(("frame", "head"), None)
    return jax.shard_map(
        on_device, mesh=mesh, in_specs=in_specs, out_specs=out_specs, check_vma=False
    )
```

```python
import functools
import math

import jax
import jax.numpy as jnp
from jax import lax
from jax.experimental import pallas as pl
from jax.experimental.pallas import tpu as pltpu
from jax.sharding import PartitionSpec as P

HD = 128
BLK = 64
BF = 8
G = 4
SLOTS = 32
GB = G * BF
FT = BF * BLK
LOW = -1e30
C = math.log2(math.e) / math.sqrt(HD)
VMEM = 56 * 1024 * 1024


STAGES = ((0, 1), (1, 2))

PIECES = ((-1, 18), (1, 18), (-2, 8), (2, 8), (-4, 8), (4, 8), (8, 8))
FAR = ((2, 20), (3, 22), (4, 24), (5, 26))
STARTS = [sum(count for _, count in PIECES[:i]) for i in range(len(PIECES) + 1)]


def span(piece, first, count):
    return [(piece, first + j) for j in range(count)]


NEAR = (
    span(0, 0, 12) + span(0, 16, 2) + [(1, "zero0"), (1, "zero1")],
    span(0, 0, 8) + span(0, 14, 2) + span(1, 12, 2),
    span(1, 0, 8) + span(0, 12, 2) + span(1, 14, 2),
    span(1, 0, 12) + [(0, "three0"), (0, "three1")] + span(1, 16, 2),
)
READS = [near + [(2 + n, 2 * i + r) for n in range(5) for r in range(2)] for i, near in enumerate(NEAR)]
EXT = max(len(reads) for reads in READS)
NAMES = ("zero0", "zero1", "three0", "three1")


def smem():
    return pl.BlockSpec(memory_space=pltpu.SMEM)


def hbm():
    return pl.BlockSpec(memory_space=pl.ANY)


def line_pairs(frames, shift):
    return [(f, f // G * G + (f + shift) % G) for f in range(frames)]


def group_pairs(frames, distance):
    return [(f, f + G * distance) for f in range(frames) if 0 <= f + G * distance < frames]


def swap_pairs(frames):
    return [(f, f ^ (frames // 2)) for f in range(frames)]


def plan_kernel(groups, where, masks, send, numbers, ids, own):
    a = where[1]

    def wanted(piece, group, put):
        def entry(frame, row, column):
            return masks[((group * G + frame) * BF + row) * SLOTS + column]

        below, above = (group - 1) * GB, (group + 1) * GB

        def pair(at, frame, column):
            for r in range(2):
                put(at + r, entry(frame, 0, column + r))

        def distinct(frame, column, first):
            bits = jnp.int32(0)
            for row in range(BF):
                for r in range(2):
                    offset = entry(frame, row, column + r) - first
                    inside = (offset >= 0) & (offset < BF)
                    bits = bits | jnp.where(inside, jnp.int32(1) << jnp.clip(offset, 0, BF - 1), 0)
            for c in range(4):
                put(8 + c, first)
            count = jnp.int32(0)
            for j in range(BF):
                here = (bits >> j) & 1

                @pl.when((here == 1) & (count < 4))
                def _(count=count, j=j):
                    put(8 + count, first + j)

                count = count + here

        if piece == 0:
            for j in range(BF):
                put(j, below + 3 * BF + j)
            distinct(0, 12, below + 2 * BF)
            for n, frame in enumerate((2, 1, 0)):
                pair(12 + 2 * n, frame, 16)
        elif piece == 1:
            for j in range(BF):
                put(j, above + j)
            distinct(3, 14, above + BF)
            for n, frame in enumerate((1, 2, 3)):
                pair(12 + 2 * n, frame, 18)
        elif piece < 6:
            column = dict(FAR)[piece]
            for frame in range(G):
                pair(2 * frame, frame, column)
        else:
            for frame in range(G):
                for r in range(2):
                    put(2 * frame + r, jnp.maximum(entry(frame, 0, 28 + r), entry(frame, 0, 30 + r)))

    for p, (distance, _) in enumerate(PIECES):
        other = jnp.where(a < groups // 2, a + groups // 2, a - groups // 2) if distance == 8 else a - distance
        other = jnp.clip(other, 0, groups - 1)

        def put_send(at, block, p=p):
            send[STARTS[p] + at] = jnp.clip(block - a * GB, 0, GB - 1)

        def put_own(at, block, p=p):
            own[STARTS[p] + at] = block

        wanted(p, other, put_send)
        wanted(p, a, put_own)
    for r in range(2):
        zero = masks[(a * G * BF) * SLOTS + 18 + r]
        three = masks[((a * G + 3) * BF) * SLOTS + 16 + r]
        numbers[r] = jnp.clip(zero - (a + 1) * GB, 0, BF - 1)
        numbers[2 + r] = jnp.clip(three - (a - 1) * GB - 3 * BF, 0, BF - 1)
        ids[14 + r] = zero
        ids[3 * EXT + 12 + r] = three
    for frame, reads in enumerate(READS):
        for e in range(EXT):
            if e >= len(reads):
                ids[frame * EXT + e] = -1
            elif reads[e][1] not in NAMES:
                ids[frame * EXT + e] = own[STARTS[reads[e][0]] + reads[e][1]]


def plan(groups, where, masks):
    shapes = [jax.ShapeDtypeStruct((count,), jnp.int32) for count in (STARTS[-1], len(NAMES), G * EXT)]
    return pl.pallas_call(
        functools.partial(plan_kernel, groups),
        in_specs=[smem()] * 2,
        out_specs=[smem()] * 3,
        out_shape=shapes,
        scratch_shapes=[pltpu.SMEM((STARTS[-1],), jnp.int32)],
    )(where, masks)


def split_kernel(takes, where, *refs):
    n = len(takes)
    sources, outs, sems = refs[:n], refs[n : n + G], refs[-1]
    y = where[0]
    share = sources[0].shape[1] // G
    for s in range(G):
        to = 0
        for source, (first, heads) in zip(sources, takes):
            column = pl.multiple_of(lax.rem(y + s, G) * share + first * HD, HD)
            pltpu.make_async_copy(
                source.at[:, pl.ds(column, heads * HD)], outs[s].at[:, pl.ds(to, heads * HD)], sems.at[s]
            ).start()
            to += heads * HD
    for s in range(G):
        pltpu.make_async_copy(outs[s], outs[s], sems.at[s]).wait()


def split(where, sources, takes):
    width = sum(heads for _, heads in takes) * HD
    shape = jax.ShapeDtypeStruct((sources[0].shape[0], width), sources[0].dtype)
    return pl.pallas_call(
        functools.partial(split_kernel, takes),
        in_specs=[smem()] + [pl.BlockSpec(memory_space=pltpu.VMEM)] * len(sources),
        out_specs=[hbm()] * G,
        out_shape=[shape] * G,
        scratch_shapes=[pltpu.SemaphoreType.DMA((G,))],
        compiler_params=pltpu.CompilerParams(vmem_limit_bytes=VMEM),
    )(where, *sources)


def pack_kernel(where, send, *refs):
    parts, outs = refs[:G], refs[G : G + len(PIECES)]
    held, ins, sems = refs[G + len(PIECES) :]
    y = where[0]
    width = held.shape[1]
    loads = []
    for s, part in enumerate(parts):
        row = pl.multiple_of(lax.rem(y - s + G, G) * FT, FT)
        loads.append(pltpu.make_async_copy(part.at[:, pl.ds(0, width)], held.at[pl.ds(row, FT)], ins.at[s]))
    for load in loads:
        load.start()
    for load in loads:
        load.wait()
    for p, (_, count) in enumerate(PIECES):
        for j in range(count):
            row = pl.multiple_of(send[STARTS[p] + j] * BLK, BLK)
            pltpu.make_async_copy(held.at[pl.ds(row, BLK)], outs[p].at[j], sems.at[p]).start()
    for p in range(len(PIECES)):
        pltpu.make_async_copy(outs[p], outs[p], sems.at[p]).wait()


def pack(where, send, parts, heads):
    width = 2 * heads * HD
    dtype = parts[0].dtype
    return pl.pallas_call(
        pack_kernel,
        in_specs=[smem()] * 2 + [hbm()] * G,
        out_specs=[hbm()] * len(PIECES),
        out_shape=[jax.ShapeDtypeStruct((count, BLK, width), dtype) for _, count in PIECES],
        scratch_shapes=[
            pltpu.VMEM((G * FT, width), dtype),
            pltpu.SemaphoreType.DMA((G,)),
            pltpu.SemaphoreType.DMA((len(PIECES),)),
        ],
        compiler_params=pltpu.CompilerParams(vmem_limit_bytes=VMEM),
    )(where, send, *parts)


def marks(first):
    row = lax.broadcasted_iota(jnp.int32, (FT, HD), 0) // BLK + first
    return jnp.where(row == lax.broadcasted_iota(jnp.int32, (FT, HD), 1), 1.0, 0.0).astype(jnp.bfloat16)


def inner_kernel(where, *refs):
    q_parts, k_parts, v_parts = refs[:G], refs[G : 2 * G], refs[2 * G : 3 * G]
    bias_ref, acc_ref, sums_ref, q_all, k_all, v_all = refs[3 * G :]
    left = lax.broadcasted_iota(jnp.int32, (FT, HD), 1) < HD // 2
    y = where[0]

    @pl.when(pl.program_id(0) == 0)
    def _():
        k_all[:, HD:] = bias_ref[...]
        v_all[:, HD:] = jnp.ones((G * FT, HD), jnp.bfloat16)
        for i in range(G):
            q_all[i * FT : (i + 1) * FT, HD:] = marks(i * BF)

    for s in range(G):
        at = pl.ds(pl.multiple_of(lax.rem(y - s + G, G) * FT, FT), FT)
        q_all[at, :HD] = q_parts[s][...]
        k_all[at, :HD] = k_parts[s][...]
        v_all[at, :HD] = v_parts[s][...]
    for i in range(G):
        at = slice(i * FT, (i + 1) * FT)
        keys = slice(max(0, i - 2) * FT, min(G, i + 3) * FT)
        s = lax.dot_general(
            q_all[at, :], k_all[keys, :], (((1,), (1,)), ((), ())), preferred_element_type=jnp.float32
        )
        peak = jnp.max(s, axis=1, keepdims=True)
        raised = jnp.exp2(s * C - peak * C)
        both = jnp.dot(raised.astype(jnp.bfloat16), v_all[keys, :], preferred_element_type=jnp.float32)
        acc_ref[at, :] = both[:, :HD]
        sums_ref[at, :] = jnp.where(left, both[:, HD:], peak)


def inner(where, parts, heads, bias):
    tokens = G * FT
    column = pl.BlockSpec((tokens, HD), lambda h: (0, h))
    shape = jax.ShapeDtypeStruct((tokens, heads * HD), jnp.float32)

    def part(begin):
        return [pl.BlockSpec((FT, HD), lambda h: (0, begin + h))] * G

    return pl.pallas_call(
        inner_kernel,
        grid=(heads,),
        in_specs=[smem(), *part(2 * heads), *part(0), *part(heads), pl.BlockSpec(bias.shape, lambda h: (0, 0))],
        out_specs=[column, column],
        out_shape=[shape, shape],
        scratch_shapes=[pltpu.VMEM((tokens, 2 * HD), jnp.bfloat16)] * 3,
        compiler_params=pltpu.CompilerParams(vmem_limit_bytes=VMEM),
        cost_estimate=pl.CostEstimate(
            flops=8 * tokens * tokens * heads * HD,
            bytes_accessed=16 * tokens * heads * HD,
            transcendentals=tokens * tokens * heads,
        ),
    )(where, *parts, *parts, *parts, bias)


def outer_kernel(where, numbers, *refs):
    n = len(PIECES)
    q_parts, k_pieces, v_pieces = refs[:G], refs[G : G + n], refs[G + n : G + 2 * n]
    bias_ref, acc_ref, sums_ref, *outs = refs[G + 2 * n : 2 * G + 2 * n + 3]
    out_all, q_all, k_all, v_all = refs[2 * G + 2 * n + 3 :]
    y = where[0]

    @pl.when(pl.program_id(0) == 0)
    def _():
        k_all[:, :, HD:] = bias_ref[...]
        v_all[:, :, HD:] = jnp.ones((G, EXT * BLK, HD), jnp.bfloat16)
        for i in range(G):
            q_all[i * FT : (i + 1) * FT, HD:] = marks(0)

    for s in range(G):
        at = pl.ds(pl.multiple_of(lax.rem(y - s + G, G) * FT, FT), FT)
        q_all[at, :HD] = q_parts[s][...]
    for i, reads in enumerate(READS):
        for e, (piece, block) in enumerate(reads):
            if block in NAMES:
                block = numbers[NAMES.index(block)]
            k_all[i, e * BLK : (e + 1) * BLK, :HD] = k_pieces[piece][block]
            v_all[i, e * BLK : (e + 1) * BLK, :HD] = v_pieces[piece][block]
    for i, reads in enumerate(READS):
        at = slice(i * FT, (i + 1) * FT)
        keys = slice(0, len(reads) * BLK)
        s = lax.dot_general(
            q_all[at, :], k_all[i, keys, :], (((1,), (1,)), ((), ())), preferred_element_type=jnp.float32
        )
        before = sums_ref[at, HD // 2 : HD // 2 + 1]
        peak = jnp.maximum(jnp.max(s, axis=1, keepdims=True), before)
        raised = jnp.exp2(s * C - peak * C)
        both = jnp.dot(raised.astype(jnp.bfloat16), v_all[i, keys, :], preferred_element_type=jnp.float32)
        keep = jnp.exp2((before - peak) * C)
        total = both[:, HD:] + sums_ref[at, :1] * keep
        row = pl.multiple_of(lax.rem(y - i + G, G) * FT, FT)
        out_all[pl.ds(row, FT), :] = ((both[:, :HD] + acc_ref[at, :] * keep) / total).astype(out_all.dtype)
    for s in range(G):
        outs[s][...] = out_all[s * FT : (s + 1) * FT, :]


def outer(where, numbers, parts, heads, bias, partial, pieces):
    tokens = G * FT
    column = pl.BlockSpec((tokens, HD), lambda h: (0, h))

    def piece(kind):
        return [pl.BlockSpec((count, BLK, HD), lambda h: (0, 0, kind * heads + h)) for _, count in PIECES]

    return pl.pallas_call(
        outer_kernel,
        grid=(heads,),
        in_specs=[smem(), smem()]
        + [pl.BlockSpec((FT, HD), lambda h: (0, 2 * heads + h))] * G
        + piece(0)
        + piece(1)
        + [pl.BlockSpec(bias.shape, lambda h: (0, 0, 0)), column, column],
        out_specs=[pl.BlockSpec((FT, HD), lambda h: (0, h))] * G,
        out_shape=[jax.ShapeDtypeStruct((FT, heads * HD), jnp.bfloat16)] * G,
        scratch_shapes=[
            pltpu.VMEM((tokens, HD), jnp.bfloat16),
            pltpu.VMEM((tokens, 2 * HD), jnp.bfloat16),
            pltpu.VMEM((G, EXT * BLK, 2 * HD), jnp.bfloat16),
            pltpu.VMEM((G, EXT * BLK, 2 * HD), jnp.bfloat16),
        ],
        compiler_params=pltpu.CompilerParams(vmem_limit_bytes=VMEM),
        cost_estimate=pl.CostEstimate(
            flops=8 * tokens * EXT * BLK * heads * HD,
            bytes_accessed=16 * tokens * heads * HD,
            transcendentals=tokens * EXT * BLK * heads,
        ),
    )(where, numbers, *parts, *pieces, *pieces, bias, *partial)


def project_kernel(where, *refs):
    n = G * len(STAGES)
    parts, weight, sent_ref, kept_ref, mixed, sems = refs[:n], refs[n], *refs[n + 1 :]
    y, core = where[0], where[2]
    half = sent_ref.shape[0]
    share = mixed.shape[1] // G

    @pl.when(pl.program_id(0) == 0)
    def _():
        loads = []
        for i, (head, heads) in enumerate(STAGES):
            for s in range(G):
                column = pl.multiple_of(lax.rem(y - s + G, G) * share + head * HD, HD)
                for k, begin in enumerate((1 - core, core)):
                    loads.append(
                        pltpu.make_async_copy(
                            parts[i * G + s].at[pl.ds(pl.multiple_of(begin * half, half), half)],
                            mixed.at[pl.ds(k * half, half), pl.ds(column, heads * HD)],
                            sems.at[2 * (i * G + s) + k],
                        )
                    )
        for load in loads:
            load.start()
        for load in loads:
            load.wait()

    both = jnp.dot(mixed[...], weight[...], preferred_element_type=jnp.float32)
    sent_ref[...] = both[:half].astype(sent_ref.dtype)
    kept_ref[...] = both[half:]


def project(where, parts, weight, begin, end):
    rows, tile = parts[0].shape[0], 512
    depth = weight.shape[0]
    column = pl.BlockSpec((rows // 2, tile), lambda j: (0, j))
    return pl.pallas_call(
        project_kernel,
        grid=((end - begin) // tile,),
        in_specs=[smem()]
        + [hbm()] * len(parts)
        + [pl.BlockSpec((depth, tile), lambda j: (0, begin // tile + j))],
        out_specs=[column, column],
        out_shape=[
            jax.ShapeDtypeStruct((rows // 2, end - begin), jnp.bfloat16),
            jax.ShapeDtypeStruct((rows // 2, end - begin), jnp.float32),
        ],
        scratch_shapes=[pltpu.VMEM((rows, depth), jnp.bfloat16), pltpu.SemaphoreType.DMA((2 * len(parts),))],
        compiler_params=pltpu.CompilerParams(vmem_limit_bytes=VMEM),
        cost_estimate=pl.CostEstimate(
            flops=2 * rows * depth * (end - begin), bytes_accessed=2 * depth * (end - begin), transcendentals=0
        ),
    )(where, *parts, weight)


def after(values, *others):
    flat, tree = jax.tree.flatten(values)
    out = lax.optimization_barrier(tuple(flat) + tuple(jax.tree.leaves(others)))
    return jax.tree.unflatten(tree, out[: len(flat)])


def on_device(queries, key_rows, value_rows, block_mask, out_weight):
    n = lax.axis_size("frame")
    position = lax.axis_index("frame")
    y, a = position % G, position // G
    where = jnp.stack([y, a, lax.axis_index("head")]).astype(jnp.int32)

    def line(value, shift):
        return lax.ppermute(value, "frame", line_pairs(n, shift))

    def spread(parts):
        return [parts[0]] + [line(parts[s], s) for s in (1, 2, 3)]

    def travel(parts, which):
        pairs = {p: swap_pairs(n) if PIECES[p][0] == 8 else group_pairs(n, -PIECES[p][0]) for p in which}
        return {p: lax.ppermute(parts[p], "frame", pairs[p]) for p in which}

    masks = lax.all_to_all(
        jnp.broadcast_to(block_mask[None], (n, BF, SLOTS)), "frame", 0, 0, tiled=True
    )
    chunks = split(where, (key_rows, value_rows, queries), (STAGES[0],) * 3)
    later = split(where, after((key_rows, value_rows, queries), chunks), (STAGES[1],) * 3)
    parts = [spread(chunks), None]
    parts[1] = spread(after(later, parts[0]))
    send, numbers, ids = plan(n // G, where, after(masks.reshape(-1), later))

    rows = lax.dynamic_slice_in_dim(masks, a * G, G, 0)
    inside = a * GB + jnp.arange(GB, dtype=jnp.int32)
    hit = jnp.any(rows.reshape(1, GB, SLOTS) == inside[:, None, None], axis=2)
    bias = jnp.pad(jnp.where(hit, 0.0, LOW).astype(jnp.bfloat16), ((0, 0), (0, HD - GB)))
    bias_in = jnp.repeat(bias, BLK, axis=0)
    held = ids.reshape(G, EXT, 1, 1)
    hit = jnp.any((rows.reshape(G, 1, BF, SLOTS) == held) & (held >= 0), axis=3)
    bias = jnp.pad(jnp.where(hit, 0.0, LOW).astype(jnp.bfloat16), ((0, 0), (0, 0), (0, HD - BF)))
    bias_out = jnp.repeat(bias, BLK, axis=1)

    def within(i, *others):
        return inner(where, after(parts[i], *others), STAGES[i][1], bias_in)

    def beyond(i, partial):
        pieces = [got[i][p] for p in range(len(PIECES))]
        return outer(where, numbers, parts[i], STAGES[i][1], bias_out, partial, pieces)

    got = [{}, {}]
    first = pack(where, send, parts[0], STAGES[0][1])
    got[0].update(travel(first, (0, 1)))
    partial0 = within(0, first)
    got[0].update(travel(after(first, got[0], partial0), (2, 3)))
    second = pack(where, send, after(parts[1], partial0, got[0][0], got[0][1]), STAGES[1][1])
    got[1].update(travel(second, (0, 1)))
    got[0].update(travel(after(first, got[0][2], got[0][3]), (4, 5, 6)))
    partial1 = within(1, second)
    got[1].update(travel(after(second, partial1, got[1]), (2, 3)))
    got[1].update(travel(after(second, partial1, got[0]), (4, 5, 6)))

    outs = beyond(0, after(partial0, partial1))
    mixed = spread([outs[(G - s) % G] for s in range(G)])
    outs = beyond(1, partial1)
    mixed += spread([outs[(G - s) % G] for s in range(G)])

    columns = out_weight.shape[1]
    outs = []
    for begin in (0, columns // 2):
        sent, kept = project(where, mixed, out_weight, begin, begin + columns // 2)
        outs.append((kept, lax.ppermute(sent, "head", [(0, 1), (1, 0)])))
    return jnp.concatenate([(k + o.astype(jnp.float32)).astype(jnp.bfloat16) for k, o in outs], axis=1)


def solution(mesh):
    in_specs = (
        P("frame", "head"),
        P("frame", "head"),
        P("frame", "head"),
        P("frame", None),
        P("head", None),
    )
    out_specs = P(("frame", "head"), None)
    return jax.shard_map(
        on_device, mesh=mesh, in_specs=in_specs, out_specs=out_specs, check_vma=False
    )
```
